32 devices in a mesh: tm: 2 (over core), tile: 8 (over z, x), sect: 2 (over y).
Axes of the slice: x: 2, y: 2, z: 4, core: 2. Of those that a mesh axis runs over, the one named last changes fastest.
Arguments:
- latents: bfloat16 [2, 8, 8, 8, 4, 16], P(None, ('tm', 'sect'), 'tile'), may hold values from -400 to 400
- in_weight: bfloat16 [3, 3, 3, 16, 512], replicated, may hold values from -0.3125 to 0.3125
- gn_gain: float32 [512], replicated, may hold values from 0.1 to 1.9
- gn_shift: float32 [512], replicated, may hold values from -3 to 3
- up_weight: bfloat16 [3, 3, 3, 512, 256], replicated, may hold values from -0.0546875 to 0.0546875
Outputs:
- decoded: bfloat16 [2, 8, 8, 16, 8, 256], P('sect', 'tm', 'tile')
The draws below stay inside these ranges and needn't reach their ends.
All inputs are finite; a program needn't handle non-finite values.
Results may differ from the reference program's by a relative error of at most 0.005.
Values may be sent and summed in bfloat16 or wider, within the bound.
A program may use at most 64 MiB of HBM per device.

```python
import math
import jax
import jax.numpy as jnp
from jax import lax

LAT_CH = 16
CH = 512
OUT_CH = 256
GROUPS = 32
LH = 8
LW = 4
CLIPS = 2
FRAMES = 8
LAT_W = 32
N_TILE = 8


def draw_latents(key, part):
    key = jax.random.fold_in(key, 7)
    key_base, key_cols = jax.random.split(key, 2)
    full_shape = (CLIPS, FRAMES, LH, LAT_W, LAT_CH)
    row_frac = jnp.arange(LH, dtype=jnp.float32) / max(LH - 1, 1)
    row_scale = (10.0 ** row_frac).reshape(1, 1, LH, 1, 1)
    col_scale = jnp.exp(jax.random.uniform(key_cols, (LAT_W,), minval=0.0, maxval=math.log(10.0))).reshape(1, 1, 1, LAT_W, 1)
    base_draw = jnp.clip(jax.random.normal(key_base, full_shape), -4.0, 4.0)
    grid = base_draw * row_scale * col_scale
    strips = grid.reshape(CLIPS, FRAMES, LH, LAT_W // LW, LW, LAT_CH)
    return jnp.transpose(strips, (0, 1, 3, 2, 4, 5)).astype(jnp.bfloat16)


def centred(rng, shape, width, most, held_as=jnp.bfloat16):
    entries = width * jax.random.normal(rng, shape, jnp.float32)
    return jnp.clip(entries, min=-most, max=most).astype(held_as)


def setup_inputs(seed: int = 0) -> dict:
    streams_of = jax.random.split(jax.random.key(seed), 6)
    return {
        "latents": draw_latents(jax.random.fold_in(streams_of[5], 71), 0),
        "in_weight": centred(streams_of[1], (3, 3, 3, LAT_CH, CH), (27 * LAT_CH) ** -0.5, 0.3125),
        "gn_gain": jnp.clip(1.0 + 0.18 * jax.random.normal(streams_of[2], (CH,), jnp.float32), 0.1, 1.9),
        "gn_shift": centred(streams_of[3], (CH,), 0.5, 3.0, jnp.float32),
        "up_weight": centred(streams_of[4], (3, 3, 3, CH, OUT_CH), (27 * CH) ** -0.5, 0.0546875),
    }


EPSILON = 1e-06

def width_stack(padded):
    inner_cols = padded.shape[-2] - 2
    return jnp.concatenate([padded[..., 0:inner_cols, :], padded[..., 1:inner_cols + 1, :], padded[..., 2:inner_cols + 2, :]], axis=-1)

def causal_conv(padded, weight):
    stacked = width_stack(padded)
    batch_len, frames_in, rows_in, inner_cols, merged = stacked.shape
    out_frames = frames_in - 2
    out_rows = rows_in - 2
    out_chans = weight.shape[-1]
    kernel = weight.reshape(3, 3, merged, out_chans)
    accum_sum = jnp.zeros((batch_len * out_frames * out_rows * inner_cols, out_chans), jnp.float32)
    for tap_t in range(3):
        for tap_h in range(3):
            tap_rows = stacked[:, tap_t:tap_t + out_frames, tap_h:tap_h + out_rows].reshape(-1, merged)
            accum_sum = accum_sum + jnp.dot(tap_rows, kernel[tap_t, tap_h], preferred_element_type=jnp.float32)
    return accum_sum.reshape(batch_len, out_frames, out_rows, inner_cols, out_chans)

def upsample_twice(values):
    in_shape = values.shape
    leading = in_shape[:-3]
    rows_in, cols_in, chans = (in_shape[-3], in_shape[-2], in_shape[-1])
    grown = jnp.broadcast_to(values[..., :, None, :, None, :], leading + (rows_in, 2, cols_in, 2, chans))
    return grown.reshape(leading + (2 * rows_in, 2 * cols_in, chans))

def apply_norm(pre, group_mean, inv_std, gn_gain, gn_shift, groups):
    in_shape = pre.shape
    grouped = pre.reshape(in_shape[:-1] + (groups, in_shape[-1] // groups))
    lead_ones = (1,) * (len(in_shape) - 2)
    center = group_mean.reshape((in_shape[0],) + lead_ones + (groups, 1))
    spread = inv_std.reshape((in_shape[0],) + lead_ones + (groups, 1))
    normed = ((grouped - center) * spread).reshape(in_shape)
    return jax.nn.silu(normed * gn_gain + gn_shift).astype(jnp.bfloat16)

def reference(latents, in_weight, gn_gain, gn_shift, up_weight):
    grid = jnp.transpose(latents, (0, 1, 3, 2, 4, 5)).reshape(CLIPS, FRAMES, LH, LAT_W, LAT_CH)
    lat_padded = jnp.pad(grid, ((0, 0), (2, 0), (1, 1), (1, 1), (0, 0)))
    pre = causal_conv(lat_padded, in_weight)
    grouped = pre.reshape(CLIPS, -1, GROUPS, CH // GROUPS)
    group_mean = lax.optimization_barrier(jnp.mean(grouped, axis=(1, 3)))
    group_var = lax.optimization_barrier(jnp.mean(jnp.square(grouped - group_mean[:, None, :, None]), axis=(1, 3)))
    act = apply_norm(pre, group_mean, lax.rsqrt(group_var + EPSILON), gn_gain, gn_shift, GROUPS)
    act_padded = jnp.pad(act, ((0, 0), (2, 0), (0, 0), (0, 0), (0, 0)))

    def one_frame(frame_idx):
        window = lax.dynamic_slice_in_dim(act_padded, frame_idx, 3, 1)

        def one_clip(clip_act):
            grown = upsample_twice(clip_act)
            padded = jnp.pad(grown, ((0, 0), (1, 1), (1, 1), (0, 0)))
            return causal_conv(padded[None], up_weight)[0, 0].astype(jnp.bfloat16)
        return lax.map(one_clip, window)
    stacked = lax.map(one_frame, jnp.arange(FRAMES, dtype=jnp.int32))
    out_grid = jnp.transpose(stacked, (1, 0, 2, 3, 4))
    out_blocks = out_grid.reshape(CLIPS, FRAMES, 2 * LH, N_TILE, 2 * LW, OUT_CH)
    return jnp.transpose(out_blocks, (0, 1, 3, 2, 4, 5))
```

```python
import functools

import jax
import jax.numpy as jnp
from jax import lax
from jax.experimental import pallas as pl
from jax.experimental.pallas import tpu as pltpu
from jax.sharding import PartitionSpec as P

GROUPS = 32
EPSILON = 1e-06
MESH = pl.DeviceIdType.MESH
F32 = jnp.float32
BF16 = jnp.bfloat16


def iota(shape, dim):
    return lax.broadcasted_iota(jnp.int32, shape, dim)


def pieces(row, first, rows=8):
    high = row.astype(BF16).astype(F32)
    rest = row - high
    mid = rest.astype(BF16).astype(F32)
    low = rest - mid
    width = row.shape[-1]
    ids = iota((rows, width), 0)
    out = jnp.zeros((rows, width), F32)
    for k, part in enumerate((high, mid, low)):
        out = jnp.where(ids == first + k, jnp.broadcast_to(part, (rows, width)), out)
    return out


def kernel(
    sizes,
    lat_ref,
    w1_ref,
    gain_ref,
    shift_ref,
    up_ref,
    out_ref,
    sendbuf,
    latbuf,
    w1_buf,
    lhs1,
    pre,
    gfull,
    gsum,
    gexp,
    stats,
    raw,
    mixed,
    lhs2,
    grid_out,
    up_sem,
    lat_send,
    lat_recv,
    st_send,
    st_recv,
):
    n_tm, n_tile, n_sect = sizes
    clips, blk, _, rows, cols, lat_ch = lat_ref.shape
    chans = w1_ref.shape[-1]
    out_ch = up_ref.shape[-1]
    group = chans // GROUPS
    span = blk * n_sect
    strip = blk * rows
    frames = 2 * span
    act_f = span + 2
    act_c = cols + 2
    cell = act_f * rows
    peers = n_tm * n_tile

    tm = lax.axis_index("tm")
    q = lax.axis_index("tile")
    sect = lax.axis_index("sect")
    me = tm * n_tile + q

    ups = []
    for a in range(3):
        copy = pltpu.make_async_copy(
            up_ref.at[a], raw.at[:, :, pl.ds(a * chans, chans), :], up_sem.at[a]
        )
        copy.start()
        ups.append(copy)

    def inside(dtm, dq):
        return (tm + dtm >= 0) & (tm + dtm < n_tm) & (q + dq >= 0) & (q + dq < n_tile)

    barrier = pltpu.get_barrier_semaphore()

    def peer_of(k):
        other = lax.rem(me + k, peers)
        return (other // n_tile, lax.rem(other, n_tile), sect)

    def greet(k, carry):
        pl.semaphore_signal(barrier, inc=1, device_id=peer_of(k), device_id_type=MESH)
        return carry

    for ds in range(1, n_sect):
        for dtm in range(2):
            for dq in (-1, 0, 1):

                @pl.when(inside(-dtm, dq))
                def _(dtm=dtm, dq=dq, ds=ds):
                    pl.semaphore_signal(
                        barrier,
                        inc=1,
                        device_id=(tm - dtm, q + dq, lax.rem(sect + n_sect - ds, n_sect)),
                        device_id_type=MESH,
                    )

    lax.fori_loop(1, peers, greet, 0)

    width = 128
    x = lat_ref[:, :, 0].astype(F32)
    placed = jnp.zeros((clips * strip, 3 * width), F32)
    for j in range(cols):
        col = x[:, :, :, j, :].reshape(clips * strip, lat_ch).astype(BF16)
        r = iota((lat_ch, 3 * width), 0)
        c = iota((lat_ch, 3 * width), 1)
        hit = (c == width + (j + 2) * lat_ch + r)
        if j >= cols - 2:
            hit = hit | (c == (j - cols + 2) * lat_ch + r)
        if j < 2:
            hit = hit | (c == 2 * width + (j + 2 + cols) * lat_ch + r)
        place = jnp.where(hit, 1.0, 0.0).astype(BF16)
        placed = placed + jnp.dot(col, place, preferred_element_type=F32)
    for pos in range(3):
        sendbuf[pos] = (
            placed[:, pos * width : (pos + 1) * width].astype(BF16).reshape(clips, strip, width)
        )

    targets = n_sect - 1
    steps_tm = jnp.where(tm + 1 < n_tm, 2, 1)
    steps_q = 1 + jnp.where(q > 0, 1, 0) + jnp.where(q + 1 < n_tile, 1, 0)
    pl.semaphore_wait(barrier, peers - 1 + targets * steps_tm * steps_q)

    def lat_copy(dtm, dq, ds, src_tm, src_q, src_sect):
        clip = lax.rem(src_sect + ds, n_sect)
        pos = 1 - dq
        slot = (1 - dtm) * n_sect + src_sect
        return pltpu.make_async_remote_copy(
            src_ref=sendbuf.at[pos, clip],
            dst_ref=latbuf.at[slot, pos],
            send_sem=lat_send.at[dtm, pos, ds],
            recv_sem=lat_recv.at[slot, pos],
            device_id=(src_tm + dtm, src_q + dq, clip),
            device_id_type=MESH,
        )

    moves = [
        (dtm, dq, ds)
        for ds in reversed(range(n_sect))
        for dq in (1, -1, 0)
        for dtm in (1, 0)
        if (dtm, dq, ds) != (0, 0, 0)
    ]
    for dtm, dq, ds in moves:

        @pl.when(inside(dtm, dq))
        def _(dtm=dtm, dq=dq, ds=ds):
            lat_copy(dtm, dq, ds, tm, q, sect).start()

    latbuf[n_sect + sect, 1] = sendbuf[1, sect]
    for dtm, dq, ds in moves:

        @pl.when(jnp.logical_not(inside(-dtm, -dq)))
        def _(dtm=dtm, dq=dq, ds=ds):
            slot = (1 - dtm) * n_sect + lax.rem(sect + n_sect - ds, n_sect)
            latbuf[slot, 1 - dq] = jnp.zeros((strip, width), BF16)

    w1_buf[...] = jnp.zeros(w1_buf.shape, BF16)
    for a in range(3):
        for b in range(3):
            for e in range(3):
                w1_buf[pl.ds(a * 256 + b * 64 + e * lat_ch, lat_ch), :] = w1_ref[a, b, e]

    r = iota((chans, chans), 0)
    c = iota((chans, chans), 1)
    gfull[...] = jnp.where(r // group == c // group, 1.0, 0.0).astype(BF16)
    r = iota((chans, 128), 0)
    c = iota((chans, 128), 1)
    gsum[...] = jnp.where((r >= c * group) & (r < (c + 1) * group), 1.0, 0.0).astype(BF16)
    r = iota((128, chans), 0)
    c = iota((128, chans), 1)
    gexp[...] = jnp.where((c >= r * group) & (c < (r + 1) * group), 1.0, 0.0).astype(BF16)

    step = 16

    def mix(k, carry):
        at = pl.ds(pl.multiple_of(k * step, step), step)
        taps = [[raw[b, e, at, :].astype(F32) for e in range(3)] for b in range(3)]
        sums = [
            taps[0],
            [taps[1][e] + taps[2][e] for e in range(3)],
            [taps[0][e] + taps[1][e] for e in range(3)],
            taps[2],
        ]
        for i, row in enumerate(sums):
            if i in (1, 2):
                mixed[i, 0, at, :] = row[0].astype(BF16)
                mixed[i, 3, at, :] = row[2].astype(BF16)
            mixed[i, 1, at, :] = (row[1] + row[2]).astype(BF16)
            mixed[i, 2, at, :] = (row[0] + row[1]).astype(BF16)
        return carry

    per = chans // step
    for a in range(2):
        ups[a].wait()
        lax.fori_loop(a * per, (a + 1) * per, mix, 0)

    for dtm, dq, ds in moves:

        @pl.when(inside(-dtm, -dq))
        def _(dtm=dtm, dq=dq, ds=ds):
            src = lax.rem(sect + n_sect - ds, n_sect)
            lat_copy(dtm, dq, ds, tm - dtm, q - dq, src).wait_recv()

    cells = (
        latbuf[:, 0].astype(F32) + latbuf[:, 1].astype(F32) + latbuf[:, 2].astype(F32)
    ).reshape(frames * rows, width)
    row_id = lax.rem(iota((frames * rows, width), 0), rows)
    lane = iota((frames * rows, width), 1)
    above = jnp.where(row_id == 0, 0.0, pltpu.roll(cells, 1, 0))
    below = jnp.where(row_id == rows - 1, 0.0, pltpu.roll(cells, frames * rows - 1, 0))
    for j in range(act_c):
        back = (width - j * lat_ch) % width
        half = (width + 64 - j * lat_ch) % width
        r0 = pltpu.roll(above, back, 1) if back else above
        r1 = pltpu.roll(cells, half, 1) if half else cells
        r2 = pltpu.roll(below, back, 1) if back else below
        both = jnp.where(lane < 64, r0, r1)
        for a in range(3):
            at = pl.ds(j * cell, cell)
            lhs1[at, a * 256 : a * 256 + 128] = both[a * rows : a * rows + cell].astype(BF16)
            lhs1[at, a * 256 + 128 : a * 256 + 256] = r2[a * rows : a * rows + cell].astype(BF16)
    pre[...] = jnp.dot(lhs1[...], w1_buf[...], preferred_element_type=F32)

    count = span * rows * cols
    own = [pl.ds(j * cell + 2 * rows, span * rows) for j in range(1, cols + 1)]
    total = jnp.zeros((1, chans), F32)
    for at in own:
        total = total + jnp.sum(pre[at, :], axis=0, keepdims=True)
    scaled = total * (1.0 / (count * group))
    parts = pieces(scaled, 0)
    local = jnp.sum(
        jnp.dot(parts.astype(BF16), gfull[...], preferred_element_type=F32), axis=0, keepdims=True
    )
    square = jnp.zeros((1, chans), F32)
    for at in own:
        off = pre[at, :] - local
        square = square + jnp.sum(off * off, axis=0, keepdims=True)
    both = parts + pieces(square, 3)
    sums = jnp.dot(both.astype(BF16), gsum[...], preferred_element_type=F32)
    ids = iota(sums.shape, 0)
    local_mean = jnp.sum(jnp.where(ids < 3, sums, 0.0), axis=0, keepdims=True)
    local_sq = jnp.sum(jnp.where(ids >= 3, sums, 0.0), axis=0, keepdims=True)
    stats[me] = jnp.concatenate([local_mean, local_sq], axis=0)

    def send_stats(k, carry):
        pltpu.make_async_remote_copy(
            src_ref=stats.at[me],
            dst_ref=stats.at[me],
            send_sem=st_send,
            recv_sem=st_recv,
            device_id=peer_of(k),
            device_id_type=MESH,
        ).start()
        return carry

    lax.fori_loop(1, peers, send_stats, 0)

    ups[2].wait()
    lax.fori_loop(2 * per, 3 * per, mix, 0)

    some = stats.at[pl.ds(0, peers - 1)]
    pltpu.make_async_copy(some, some, st_recv).wait()

    all_mean = jnp.zeros((1, 128), F32)
    for p in range(peers) if peers <= 16 else ():
        all_mean = all_mean + stats[p, 0:1, :]
    if peers > 16:
        all_mean = lax.fori_loop(0, peers, lambda p, t: t + stats[p, 0:1, :], all_mean)
    all_mean = all_mean * (1.0 / peers)

    def spread(p, acc):
        off = stats[p, 0:1, :] - all_mean
        return acc + stats[p, 1:2, :] + off * off * float(count * group)

    all_sq = jnp.zeros((1, 128), F32)
    if peers <= 16:
        for p in range(peers):
            all_sq = spread(p, all_sq)
    else:
        all_sq = lax.fori_loop(0, peers, spread, all_sq)
    inv = lax.rsqrt(all_sq * (1.0 / (peers * count * group)) + EPSILON)
    wide = jnp.dot(
        (pieces(all_mean, 0) + pieces(inv, 3)).astype(BF16), gexp[...], preferred_element_type=F32
    )
    ids = iota(wide.shape, 0)
    mean_c = jnp.sum(jnp.where(ids < 3, wide, 0.0), axis=0, keepdims=True)
    inv_c = jnp.sum(jnp.where(ids >= 3, wide, 0.0), axis=0, keepdims=True)
    scale_c = inv_c * gain_ref[...]
    shift_c = shift_ref[...]

    row_id = lax.rem(iota((cell, chans), 0), rows)
    early = iota((cell, chans), 0) < 2 * rows
    dead = early & (tm == 0)
    for j in range(act_c):
        y = (pre[pl.ds(j * cell, cell), :] - mean_c) * scale_c + shift_c
        act = y / (1.0 + jnp.exp(-y))
        gone = dead
        if j == 0:
            gone = gone | (q == 0)
        if j == act_c - 1:
            gone = gone | (q == n_tile - 1)
        act = jnp.where(gone, 0.0, act)
        above = jnp.where(row_id == 0, 0.0, pltpu.roll(act, 1, 0))
        below = jnp.where(row_id == rows - 1, 0.0, pltpu.roll(act, cell - 1, 0))
        for s, moved in enumerate((above, act, below)):
            for a in range(3):
                lhs2[s, pl.ds(j * span * rows, span * rows), a * chans : (a + 1) * chans] = moved[
                    a * rows : a * rows + span * rows
                ].astype(BF16)

    def weight(i, k):
        if i in (0, 3) and k in (0, 3):
            return raw[i - i // 3, k - k // 3]
        return mixed[i, k]

    many = cols * span * rows
    for ri in range(2):
        for cj in range(2):
            acc = jnp.zeros((many, out_ch), F32)
            for u in range(2):
                for v in range(2):
                    left = lhs2[ri + u, pl.ds((cj + v) * span * rows, many), :]
                    acc = acc + jnp.dot(
                        left, weight(2 * ri + u, 2 * cj + v), preferred_element_type=F32
                    )
            for j in range(cols):
                for t in range(span):
                    part = acc[(j * span + t) * rows : (j * span + t + 1) * rows]
                    first = t * 4 * rows * cols + ri * 2 * cols + 2 * j + cj
                    for h in range(out_ch // 128):
                        grid_out[h, pl.ds(first, rows, 4 * cols), :] = part[
                            :, h * 128 : (h + 1) * 128
                        ]
    for h in range(out_ch // 128):
        out_ref[0, :, 0, :, :, h * 128 : (h + 1) * 128] = (
            grid_out[h].reshape(span, 2 * rows, 2 * cols, 128).astype(BF16)
        )

    for dtm, dq, ds in moves:

        @pl.when(inside(dtm, dq))
        def _(dtm=dtm, dq=dq, ds=ds):
            lat_copy(dtm, dq, ds, tm, q, sect).wait_send()

    pltpu.make_async_copy(some, some, st_send).wait()


def shards(sizes, latents, in_weight, gn_gain, gn_shift, up_weight):
    n_tm, n_tile, n_sect = sizes
    clips, blk, _, rows, cols, lat_ch = latents.shape
    chans, out_ch = in_weight.shape[-1], up_weight.shape[-1]
    span = blk * n_sect
    cell = (span + 2) * rows
    act_c = cols + 2
    peers = n_tm * n_tile
    vmem = pl.BlockSpec(memory_space=pltpu.VMEM)
    return pl.pallas_call(
        functools.partial(kernel, sizes),
        out_shape=jax.ShapeDtypeStruct((1, span, 1, 2 * rows, 2 * cols, out_ch), BF16),
        in_specs=[vmem, vmem, vmem, vmem, pl.BlockSpec(memory_space=pltpu.HBM)],
        out_specs=vmem,
        scratch_shapes=[
            pltpu.VMEM((3, clips, blk * rows, 128), BF16),
            pltpu.VMEM((2 * n_sect, 3, blk * rows, 128), BF16),
            pltpu.VMEM((768, chans), BF16),
            pltpu.VMEM((act_c * cell, 768), BF16),
            pltpu.VMEM((act_c * cell, chans), F32),
            pltpu.VMEM((chans, chans), BF16),
            pltpu.VMEM((chans, 128), BF16),
            pltpu.VMEM((128, chans), BF16),
            pltpu.VMEM((peers, 2, 128), F32),
            pltpu.VMEM((3, 3, 3 * chans, out_ch), BF16),
            pltpu.VMEM((4, 4, 3 * chans, out_ch), BF16),
            pltpu.VMEM((3, act_c * span * rows, 3 * chans), BF16),
            pltpu.VMEM((out_ch // 128, span * 4 * rows * cols, 128), F32),
            pltpu.SemaphoreType.DMA((3,)),
            pltpu.SemaphoreType.DMA((2, 3, n_sect)),
            pltpu.SemaphoreType.DMA((2 * n_sect, 3)),
            pltpu.SemaphoreType.DMA,
            pltpu.SemaphoreType.DMA,
        ],
        compiler_params=pltpu.CompilerParams(
            collective_id=0, has_side_effects=True, vmem_limit_bytes=56 * 1024 * 1024
        ),
        cost_estimate=pl.CostEstimate(
            flops=2_500_000_000, bytes_accessed=8_000_000, transcendentals=300_000
        ),
    )(latents, in_weight, gn_gain.reshape(1, chans), gn_shift.reshape(1, chans), up_weight)


def solution(mesh):
    sizes = (mesh.shape["tm"], mesh.shape["tile"], mesh.shape["sect"])
    placed = (P(None, ("tm", "sect"), "tile", None, None, None), P(), P(), P(), P())
    return jax.shard_map(
        functools.partial(shards, sizes),
        mesh=mesh,
        in_specs=placed,
        out_specs=P("sect", "tm", "tile", None, None, None),
        check_vma=False,
    )
```

```python
import functools

import jax
import jax.numpy as jnp
from jax import lax
from jax.experimental import pallas as pl
from jax.experimental.pallas import tpu as pltpu
from jax.sharding import PartitionSpec as P

GROUPS = 32
EPSILON = 1e-06
MESH = pl.DeviceIdType.MESH
F32 = jnp.float32
BF16 = jnp.bfloat16


def iota(shape, dim):
    return lax.broadcasted_iota(jnp.int32, shape, dim)


def pieces(row, first, rows=8):
    high = row.astype(BF16).astype(F32)
    rest = row - high
    mid = rest.astype(BF16).astype(F32)
    low = rest - mid
    width = row.shape[-1]
    ids = iota((rows, width), 0)
    out = jnp.zeros((rows, width), F32)
    for k, part in enumerate((high, mid, low)):
        out = jnp.where(ids == first + k, jnp.broadcast_to(part, (rows, width)), out)
    return out


def kernel(
    sizes,
    lat_hbm,
    w1_hbm,
    gain_hbm,
    shift_hbm,
    up_ref,
    out_ref,
    lat_ref,
    gain_ref,
    shift_ref,
    sendbuf,
    latbuf,
    w1_buf,
    lhs1,
    pre,
    gfull,
    gsum,
    gexp,
    stats,
    raw,
    mixed,
    lhs2,
    grid_out,
    in_sem,
    up_sem,
    lat_send,
    lat_recv,
    st_send,
    st_recv,
):
    n_tm, n_tile, n_sect = sizes
    clips, blk, _, rows, cols, lat_ch = lat_hbm.shape
    chans = w1_hbm.shape[-1]
    out_ch = up_ref.shape[-1]
    group = chans // GROUPS
    span = blk * n_sect
    strip = blk * rows
    frames = 2 * span
    act_f = span + 2
    act_c = cols + 2
    cell = act_f * rows
    peers = n_tm * n_tile

    tm = lax.axis_index("tm")
    q = lax.axis_index("tile")
    sect = lax.axis_index("sect")
    me = tm * n_tile + q

    loads = [
        pltpu.make_async_copy(lat_hbm, lat_ref, in_sem.at[0]),
        pltpu.make_async_copy(w1_hbm, w1_buf.at[:, pl.ds(0, 3), pl.ds(0, 3)], in_sem.at[1]),
        pltpu.make_async_copy(gain_hbm, gain_ref, in_sem.at[2]),
        pltpu.make_async_copy(shift_hbm, shift_ref, in_sem.at[3]),
    ]
    loads[0].start()

    def inside(dtm, dq):
        return (tm + dtm >= 0) & (tm + dtm < n_tm) & (q + dq >= 0) & (q + dq < n_tile)

    barrier = pltpu.get_barrier_semaphore()

    def peer_of(k):
        other = lax.rem(me + k, peers)
        return (other // n_tile, lax.rem(other, n_tile), sect)

    far = sorted(range(n_tile), key=lambda d: -min(d, n_tile - d))
    order = [d + c * n_tile for d in far for c in range(n_tm - 1, -1, -1) if d + c]

    def each_peer(do):
        if peers <= 16:
            for k in order:
                do(k)
        else:

            def body(k, carry):
                do(k)
                return carry

            lax.fori_loop(1, peers, body, 0)

    def greet(k):
        pl.semaphore_signal(barrier, inc=1, device_id=peer_of(k), device_id_type=MESH)

    each_peer(greet)
    for ds in range(1, n_sect):
        for dtm in range(2):
            for dq in (-1, 0, 1):

                @pl.when(inside(-dtm, dq))
                def _(dtm=dtm, dq=dq, ds=ds):
                    pl.semaphore_signal(
                        barrier,
                        inc=1,
                        device_id=(tm - dtm, q + dq, lax.rem(sect + n_sect - ds, n_sect)),
                        device_id_type=MESH,
                    )

    for load in loads[1:]:
        load.start()
    ups = []
    for a in range(3):
        copy = pltpu.make_async_copy(
            up_ref.at[a], raw.at[:, :, pl.ds(a * chans, chans), :], up_sem.at[a]
        )
        copy.start()
        ups.append(copy)

    width = 128
    loads[0].wait()
    x = lat_ref[:, :, 0].astype(F32)
    placed = jnp.zeros((clips * strip, 3 * width), F32)
    for j in range(cols):
        col = x[:, :, :, j, :].reshape(clips * strip, lat_ch).astype(BF16)
        r = iota((lat_ch, 3 * width), 0)
        c = iota((lat_ch, 3 * width), 1)
        hit = (c == width + (j + 2) * lat_ch + r)
        if j >= cols - 2:
            hit = hit | (c == (j - cols + 2) * lat_ch + r)
        if j < 2:
            hit = hit | (c == 2 * width + (j + 2 + cols) * lat_ch + r)
        place = jnp.where(hit, 1.0, 0.0).astype(BF16)
        placed = placed + jnp.dot(col, place, preferred_element_type=F32)
    for pos in range(3):
        sendbuf[pos] = (
            placed[:, pos * width : (pos + 1) * width].astype(BF16).reshape(clips, strip, width)
        )

    targets = n_sect - 1
    steps_tm = jnp.where(tm + 1 < n_tm, 2, 1)
    steps_q = 1 + jnp.where(q > 0, 1, 0) + jnp.where(q + 1 < n_tile, 1, 0)
    pl.semaphore_wait(barrier, peers - 1 + targets * steps_tm * steps_q)

    def lat_copy(dtm, dq, ds, src_tm, src_q, src_sect):
        clip = lax.rem(src_sect + ds, n_sect)
        pos = 1 - dq
        slot = (1 - dtm) * n_sect + src_sect
        return pltpu.make_async_remote_copy(
            src_ref=sendbuf.at[pos, clip],
            dst_ref=latbuf.at[slot, pos],
            send_sem=lat_send.at[dtm, pos, ds],
            recv_sem=lat_recv.at[slot, pos],
            device_id=(src_tm + dtm, src_q + dq, clip),
            device_id_type=MESH,
        )

    moves = [
        (dtm, dq, ds)
        for ds in reversed(range(n_sect))
        for dq in (1, -1, 0)
        for dtm in (1, 0)
        if (dtm, dq, ds) != (0, 0, 0)
    ]
    for dtm, dq, ds in moves:

        @pl.when(inside(dtm, dq))
        def _(dtm=dtm, dq=dq, ds=ds):
            lat_copy(dtm, dq, ds, tm, q, sect).start()

    latbuf[n_sect + sect, 1] = sendbuf[1, sect]
    for dtm, dq, ds in moves:

        @pl.when(jnp.logical_not(inside(-dtm, -dq)))
        def _(dtm=dtm, dq=dq, ds=ds):
            slot = (1 - dtm) * n_sect + lax.rem(sect + n_sect - ds, n_sect)
            latbuf[slot, 1 - dq] = jnp.zeros((strip, width), BF16)

    w1_buf[:, 3] = jnp.zeros((3, 4, lat_ch, chans), BF16)
    w1_buf[:, 0:3, 3] = jnp.zeros((3, 3, lat_ch, chans), BF16)

    r = iota((chans, chans), 0)
    c = iota((chans, chans), 1)
    gfull[...] = jnp.where(r // group == c // group, 1.0, 0.0).astype(BF16)
    r = iota((chans, 128), 0)
    c = iota((chans, 128), 1)
    gsum[...] = jnp.where((r >= c * group) & (r < (c + 1) * group), 1.0, 0.0).astype(BF16)
    r = iota((128, chans), 0)
    c = iota((128, chans), 1)
    gexp[...] = jnp.where((c >= r * group) & (c < (r + 1) * group), 1.0, 0.0).astype(BF16)

    step = 16

    def mix(k, carry):
        at = pl.ds(pl.multiple_of(k * step, step), step)
        taps = [[raw[b, e, at, :].astype(F32) for e in range(3)] for b in range(3)]
        sums = [
            taps[0],
            [taps[1][e] + taps[2][e] for e in range(3)],
            [taps[0][e] + taps[1][e] for e in range(3)],
            taps[2],
        ]
        for i, row in enumerate(sums):
            if i in (1, 2):
                mixed[i, 0, at, :] = row[0].astype(BF16)
                mixed[i, 3, at, :] = row[2].astype(BF16)
            mixed[i, 1, at, :] = (row[1] + row[2]).astype(BF16)
            mixed[i, 2, at, :] = (row[0] + row[1]).astype(BF16)
        return carry

    per = chans // step
    for a in range(2):
        ups[a].wait()
        lax.fori_loop(a * per, (a + 1) * per, mix, 0)

    for dtm, dq, ds in moves:

        @pl.when(inside(-dtm, -dq))
        def _(dtm=dtm, dq=dq, ds=ds):
            src = lax.rem(sect + n_sect - ds, n_sect)
            lat_copy(dtm, dq, ds, tm - dtm, q - dq, src).wait_recv()

    cells = (
        latbuf[:, 0].astype(F32) + latbuf[:, 1].astype(F32) + latbuf[:, 2].astype(F32)
    ).reshape(frames * rows, width)
    row_id = lax.rem(iota((frames * rows, width), 0), rows)
    lane = iota((frames * rows, width), 1)
    above = jnp.where(row_id == 0, 0.0, pltpu.roll(cells, 1, 0))
    below = jnp.where(row_id == rows - 1, 0.0, pltpu.roll(cells, frames * rows - 1, 0))
    for j in range(act_c):
        back = (width - j * lat_ch) % width
        half = (width + 64 - j * lat_ch) % width
        r0 = pltpu.roll(above, back, 1) if back else above
        r1 = pltpu.roll(cells, half, 1) if half else cells
        r2 = pltpu.roll(below, back, 1) if back else below
        both = jnp.where(lane < 64, r0, r1)
        for a in range(3):
            at = pl.ds(j * cell, cell)
            lhs1[at, a * 256 : a * 256 + 128] = both[a * rows : a * rows + cell].astype(BF16)
            lhs1[at, a * 256 + 128 : a * 256 + 256] = r2[a * rows : a * rows + cell].astype(BF16)
    loads[1].wait()
    w1 = w1_buf[...].reshape(768, chans)
    pre[...] = jnp.dot(lhs1[...], w1, preferred_element_type=F32)

    count = span * rows * cols
    own = [pl.ds(j * cell + 2 * rows, span * rows) for j in range(1, cols + 1)]
    total = jnp.zeros((1, chans), F32)
    for at in own:
        total = total + jnp.sum(pre[at, :], axis=0, keepdims=True)
    scaled = total * (1.0 / (count * group))
    parts = pieces(scaled, 0)
    local = jnp.sum(
        jnp.dot(parts.astype(BF16), gfull[...], preferred_element_type=F32), axis=0, keepdims=True
    )
    square = jnp.zeros((1, chans), F32)
    for at in own:
        off = pre[at, :] - local
        square = square + jnp.sum(off * off, axis=0, keepdims=True)
    both = parts + pieces(square, 3)
    sums = jnp.dot(both.astype(BF16), gsum[...], preferred_element_type=F32)
    ids = iota(sums.shape, 0)
    local_mean = jnp.sum(jnp.where(ids < 3, sums, 0.0), axis=0, keepdims=True)
    local_sq = jnp.sum(jnp.where(ids >= 3, sums, 0.0), axis=0, keepdims=True)
    stats[me] = jnp.concatenate([local_mean, local_sq], axis=0)

    def send_stats(k):
        pltpu.make_async_remote_copy(
            src_ref=stats.at[me],
            dst_ref=stats.at[me],
            send_sem=st_send,
            recv_sem=st_recv,
            device_id=peer_of(k),
            device_id_type=MESH,
        ).start()

    each_peer(send_stats)

    ups[2].wait()
    lax.fori_loop(2 * per, 3 * per, mix, 0)

    some = stats.at[pl.ds(0, peers - 1)]
    pltpu.make_async_copy(some, some, st_recv).wait()

    all_mean = jnp.zeros((1, 128), F32)
    for p in range(peers) if peers <= 16 else ():
        all_mean = all_mean + stats[p, 0:1, :]
    if peers > 16:
        all_mean = lax.fori_loop(0, peers, lambda p, t: t + stats[p, 0:1, :], all_mean)
    all_mean = all_mean * (1.0 / peers)

    def spread(p, acc):
        off = stats[p, 0:1, :] - all_mean
        return acc + stats[p, 1:2, :] + off * off * float(count * group)

    all_sq = jnp.zeros((1, 128), F32)
    if peers <= 16:
        for p in range(peers):
            all_sq = spread(p, all_sq)
    else:
        all_sq = lax.fori_loop(0, peers, spread, all_sq)
    inv = lax.rsqrt(all_sq * (1.0 / (peers * count * group)) + EPSILON)
    wide = jnp.dot(
        (pieces(all_mean, 0) + pieces(inv, 3)).astype(BF16), gexp[...], preferred_element_type=F32
    )
    ids = iota(wide.shape, 0)
    mean_c = jnp.sum(jnp.where(ids < 3, wide, 0.0), axis=0, keepdims=True)
    inv_c = jnp.sum(jnp.where(ids >= 3, wide, 0.0), axis=0, keepdims=True)
    loads[2].wait()
    loads[3].wait()
    scale_c = inv_c * gain_ref[...]
    shift_c = shift_ref[...]

    row_id = lax.rem(iota((cell, chans), 0), rows)
    early = iota((cell, chans), 0) < 2 * rows
    dead = early & (tm == 0)
    for j in range(act_c):
        y = (pre[pl.ds(j * cell, cell), :] - mean_c) * scale_c + shift_c
        act = y / (1.0 + jnp.exp(-y))
        gone = dead
        if j == 0:
            gone = gone | (q == 0)
        if j == act_c - 1:
            gone = gone | (q == n_tile - 1)
        act = jnp.where(gone, 0.0, act)
        above = jnp.where(row_id == 0, 0.0, pltpu.roll(act, 1, 0))
        below = jnp.where(row_id == rows - 1, 0.0, pltpu.roll(act, cell - 1, 0))
        for s, moved in enumerate((above, act, below)):
            for a in range(3):
                lhs2[s, pl.ds(j * span * rows, span * rows), a * chans : (a + 1) * chans] = moved[
                    a * rows : a * rows + span * rows
                ].astype(BF16)

    def weight(i, k):
        if i in (0, 3) and k in (0, 3):
            return raw[i - i // 3, k - k // 3]
        return mixed[i, k]

    many = cols * span * rows
    for ri in range(2):
        for cj in range(2):
            acc = jnp.zeros((many, out_ch), F32)
            for u in range(2):
                for v in range(2):
                    left = lhs2[ri + u, pl.ds((cj + v) * span * rows, many), :]
                    acc = acc + jnp.dot(
                        left, weight(2 * ri + u, 2 * cj + v), preferred_element_type=F32
                    )
            for j in range(cols):
                for t in range(span):
                    part = acc[(j * span + t) * rows : (j * span + t + 1) * rows]
                    first = t * 4 * rows * cols + ri * 2 * cols + 2 * j + cj
                    for h in range(out_ch // 128):
                        grid_out[h, pl.ds(first, rows, 4 * cols), :] = part[
                            :, h * 128 : (h + 1) * 128
                        ]
    for h in range(out_ch // 128):
        out_ref[0, :, 0, :, :, h * 128 : (h + 1) * 128] = (
            grid_out[h].reshape(span, 2 * rows, 2 * cols, 128).astype(BF16)
        )

    for dtm, dq, ds in moves:

        @pl.when(inside(dtm, dq))
        def _(dtm=dtm, dq=dq, ds=ds):
            lat_copy(dtm, dq, ds, tm, q, sect).wait_send()

    pltpu.make_async_copy(some, some, st_send).wait()


def shards(sizes, latents, in_weight, gn_gain, gn_shift, up_weight):
    n_tm, n_tile, n_sect = sizes
    clips, blk, _, rows, cols, lat_ch = latents.shape
    chans, out_ch = in_weight.shape[-1], up_weight.shape[-1]
    span = blk * n_sect
    cell = (span + 2) * rows
    act_c = cols + 2
    peers = n_tm * n_tile
    vmem = pl.BlockSpec(memory_space=pltpu.VMEM)
    return pl.pallas_call(
        functools.partial(kernel, sizes),
        out_shape=jax.ShapeDtypeStruct((1, span, 1, 2 * rows, 2 * cols, out_ch), BF16),
        in_specs=[pl.BlockSpec(memory_space=pltpu.HBM)] * 5,
        out_specs=vmem,
        scratch_shapes=[
            pltpu.VMEM(latents.shape, BF16),
            pltpu.VMEM((1, chans), F32),
            pltpu.VMEM((1, chans), F32),
            pltpu.VMEM((3, clips, blk * rows, 128), BF16),
            pltpu.VMEM((2 * n_sect, 3, blk * rows, 128), BF16),
            pltpu.VMEM((3, 4, 4, in_weight.shape[3], chans), BF16),
            pltpu.VMEM((act_c * cell, 768), BF16),
            pltpu.VMEM((act_c * cell, chans), F32),
            pltpu.VMEM((chans, chans), BF16),
            pltpu.VMEM((chans, 128), BF16),
            pltpu.VMEM((128, chans), BF16),
            pltpu.VMEM((peers, 2, 128), F32),
            pltpu.VMEM((3, 3, 3 * chans, out_ch), BF16),
            pltpu.VMEM((4, 4, 3 * chans, out_ch), BF16),
            pltpu.VMEM((3, act_c * span * rows, 3 * chans), BF16),
            pltpu.VMEM((out_ch // 128, span * 4 * rows * cols, 128), F32),
            pltpu.SemaphoreType.DMA((4,)),
            pltpu.SemaphoreType.DMA((3,)),
            pltpu.SemaphoreType.DMA((2, 3, n_sect)),
            pltpu.SemaphoreType.DMA((2 * n_sect, 3)),
            pltpu.SemaphoreType.DMA,
            pltpu.SemaphoreType.DMA,
        ],
        compiler_params=pltpu.CompilerParams(
            collective_id=0, has_side_effects=True, vmem_limit_bytes=56 * 1024 * 1024
        ),
        cost_estimate=pl.CostEstimate(
            flops=2_500_000_000, bytes_accessed=8_000_000, transcendentals=300_000
        ),
    )(latents, in_weight, gn_gain.reshape(1, chans), gn_shift.reshape(1, chans), up_weight)


def solution(mesh):
    sizes = (mesh.shape["tm"], mesh.shape["tile"], mesh.shape["sect"])
    placed = (P(None, ("tm", "sect"), "tile", None, None, None), P(), P(), P(), P())
    return jax.shard_map(
        functools.partial(shards, sizes),
        mesh=mesh,
        in_specs=placed,
        out_specs=P("sect", "tm", "tile", None, None, None),
        check_vma=False,
    )
```

```python
import functools

import jax
import jax.numpy as jnp
from jax import lax
from jax.experimental import pallas as pl
from jax.experimental.pallas import tpu as pltpu
from jax.sharding import PartitionSpec as P

GROUPS = 32
EPSILON = 1e-06
MESH = pl.DeviceIdType.MESH
F32 = jnp.float32
BF16 = jnp.bfloat16


def iota(shape, dim):
    return lax.broadcasted_iota(jnp.int32, shape, dim)


def pieces(row, first, rows=8):
    high = row.astype(BF16).astype(F32)
    rest = row - high
    mid = rest.astype(BF16).astype(F32)
    low = rest - mid
    width = row.shape[-1]
    ids = iota((rows, width), 0)
    out = jnp.zeros((rows, width), F32)
    for k, part in enumerate((high, mid, low)):
        out = jnp.where(ids == first + k, jnp.broadcast_to(part, (rows, width)), out)
    return out


def kernel(
    sizes,
    lat_hbm,
    w1_hbm,
    gain_hbm,
    shift_hbm,
    up_ref,
    out_ref,
    lat_ref,
    gain_ref,
    shift_ref,
    sendbuf,
    latbuf,
    w1_buf,
    lhs1,
    pre,
    gfull,
    gsum,
    gexp,
    stats,
    raw,
    mixed,
    lhs2,
    grid_out,
    in_sem,
    up_sem,
    lat_send,
    lat_recv,
    st_send,
    st_recv,
):
    n_tm, n_tile, n_sect = sizes
    clips, blk, _, rows, cols, lat_ch = lat_hbm.shape
    chans = w1_hbm.shape[-1]
    out_ch = up_ref.shape[-1]
    group = chans // GROUPS
    span = blk * n_sect
    strip = blk * rows
    frames = 2 * span
    act_f = span + 2
    act_c = cols + 2
    cell = act_f * rows
    peers = n_tm * n_tile

    tm = lax.axis_index("tm")
    q = lax.axis_index("tile")
    sect = lax.axis_index("sect")
    me = tm * n_tile + q

    loads = [
        pltpu.make_async_copy(lat_hbm, lat_ref, in_sem.at[0]),
        pltpu.make_async_copy(w1_hbm, w1_buf.at[:, pl.ds(0, 3), pl.ds(0, 3)], in_sem.at[1]),
        pltpu.make_async_copy(gain_hbm, gain_ref, in_sem.at[2]),
        pltpu.make_async_copy(shift_hbm, shift_ref, in_sem.at[3]),
    ]
    loads[0].start()

    def inside(dtm, dq):
        return (tm + dtm >= 0) & (tm + dtm < n_tm) & (q + dq >= 0) & (q + dq < n_tile)

    barrier = pltpu.get_barrier_semaphore()

    def peer_of(k):
        other = lax.rem(me + k, peers)
        return (other // n_tile, lax.rem(other, n_tile), sect)

    far = sorted(range(n_tile), key=lambda d: -min(d, n_tile - d))
    order = [d + c * n_tile for d in far for c in range(n_tm - 1, -1, -1) if d + c]

    def each_peer(do):
        if peers <= 16:
            for k in order:
                do(k)
        else:

            def body(k, carry):
                do(k)
                return carry

            lax.fori_loop(1, peers, body, 0)

    def greet(k):
        pl.semaphore_signal(barrier, inc=1, device_id=peer_of(k), device_id_type=MESH)

    each_peer(greet)
    for ds in range(1, n_sect):
        for dtm in range(2):
            for dq in (-1, 0, 1):

                @pl.when(inside(-dtm, dq))
                def _(dtm=dtm, dq=dq, ds=ds):
                    pl.semaphore_signal(
                        barrier,
                        inc=1,
                        device_id=(tm - dtm, q + dq, lax.rem(sect + n_sect - ds, n_sect)),
                        device_id_type=MESH,
                    )

    for load in loads[1:]:
        load.start()
    ups = []
    for a in range(3):
        copy = pltpu.make_async_copy(
            up_ref.at[a], raw.at[:, :, pl.ds(a * chans, chans), :], up_sem.at[a]
        )
        copy.start()
        ups.append(copy)

    width = 128
    loads[0].wait()
    x = lat_ref[:, :, 0].astype(F32)
    placed = jnp.zeros((clips * strip, 3 * width), F32)
    for j in range(cols):
        col = x[:, :, :, j, :].reshape(clips * strip, lat_ch).astype(BF16)
        r = iota((lat_ch, 3 * width), 0)
        c = iota((lat_ch, 3 * width), 1)
        hit = (c == width + (j + 2) * lat_ch + r)
        if j >= cols - 2:
            hit = hit | (c == (j - cols + 2) * lat_ch + r)
        if j < 2:
            hit = hit | (c == 2 * width + (j + 2 + cols) * lat_ch + r)
        place = jnp.where(hit, 1.0, 0.0).astype(BF16)
        placed = placed + jnp.dot(col, place, preferred_element_type=F32)
    for pos in range(3):
        sendbuf[pos] = (
            placed[:, pos * width : (pos + 1) * width].astype(BF16).reshape(clips, strip, width)
        )

    targets = n_sect - 1
    steps_tm = jnp.where(tm + 1 < n_tm, 2, 1)
    steps_q = 1 + jnp.where(q > 0, 1, 0) + jnp.where(q + 1 < n_tile, 1, 0)
    pl.semaphore_wait(barrier, peers - 1 + targets * steps_tm * steps_q)

    def lat_copy(dtm, dq, ds, src_tm, src_q, src_sect):
        clip = lax.rem(src_sect + ds, n_sect)
        pos = 1 - dq
        slot = (1 - dtm) * n_sect + src_sect
        return pltpu.make_async_remote_copy(
            src_ref=sendbuf.at[pos, clip],
            dst_ref=latbuf.at[slot, pos],
            send_sem=lat_send.at[dtm, pos, ds],
            recv_sem=lat_recv.at[slot, pos],
            device_id=(src_tm + dtm, src_q + dq, clip),
            device_id_type=MESH,
        )

    moves = [
        (dtm, dq, ds)
        for ds in reversed(range(n_sect))
        for dq in (1, -1, 0)
        for dtm in (1, 0)
        if (dtm, dq, ds) != (0, 0, 0)
    ]
    for dtm, dq, ds in moves:

        @pl.when(inside(dtm, dq))
        def _(dtm=dtm, dq=dq, ds=ds):
            lat_copy(dtm, dq, ds, tm, q, sect).start()

    latbuf[n_sect + sect, 1] = sendbuf[1, sect]
    for dtm, dq, ds in moves:

        @pl.when(jnp.logical_not(inside(-dtm, -dq)))
        def _(dtm=dtm, dq=dq, ds=ds):
            slot = (1 - dtm) * n_sect + lax.rem(sect + n_sect - ds, n_sect)
            latbuf[slot, 1 - dq] = jnp.zeros((strip, width), BF16)

    w1_buf[:, 3] = jnp.zeros((3, 4, lat_ch, chans), BF16)
    w1_buf[:, 0:3, 3] = jnp.zeros((3, 3, lat_ch, chans), BF16)

    r = iota((chans, chans), 0)
    c = iota((chans, chans), 1)
    gfull[...] = jnp.where(r // group == c // group, 1.0, 0.0).astype(BF16)
    r = iota((chans, 128), 0)
    c = iota((chans, 128), 1)
    gsum[...] = jnp.where((r >= c * group) & (r < (c + 1) * group), 1.0, 0.0).astype(BF16)
    r = iota((128, chans), 0)
    c = iota((128, chans), 1)
    gexp[...] = jnp.where((c >= r * group) & (c < (r + 1) * group), 1.0, 0.0).astype(BF16)

    step = 16

    def mix(k, carry):
        at = pl.ds(pl.multiple_of(k * step, step), step)
        taps = [[raw[b, e, at, :].astype(F32) for e in range(3)] for b in range(3)]
        sums = [
            taps[0],
            [taps[1][e] + taps[2][e] for e in range(3)],
            [taps[0][e] + taps[1][e] for e in range(3)],
            taps[2],
        ]
        for i, row in enumerate(sums):
            if i in (1, 2):
                mixed[i, 0, at, :] = row[0].astype(BF16)
                mixed[i, 3, at, :] = row[2].astype(BF16)
            mixed[i, 1, at, :] = (row[1] + row[2]).astype(BF16)
            mixed[i, 2, at, :] = (row[0] + row[1]).astype(BF16)
        return carry

    per = chans // step
    for a in range(2):
        ups[a].wait()
        lax.fori_loop(a * per, (a + 1) * per, mix, 0)

    for dtm, dq, ds in moves:

        @pl.when(inside(-dtm, -dq))
        def _(dtm=dtm, dq=dq, ds=ds):
            src = lax.rem(sect + n_sect - ds, n_sect)
            lat_copy(dtm, dq, ds, tm - dtm, q - dq, src).wait_recv()

    cells = (
        latbuf[:, 0].astype(F32) + latbuf[:, 1].astype(F32) + latbuf[:, 2].astype(F32)
    ).reshape(frames * rows, width)
    row_id = lax.rem(iota((frames * rows, width), 0), rows)
    lane = iota((frames * rows, width), 1)
    above = jnp.where(row_id == 0, 0.0, pltpu.roll(cells, 1, 0))
    below = jnp.where(row_id == rows - 1, 0.0, pltpu.roll(cells, frames * rows - 1, 0))
    for j in range(act_c):
        back = (width - j * lat_ch) % width
        half = (width + 64 - j * lat_ch) % width
        r0 = pltpu.roll(above, back, 1) if back else above
        r1 = pltpu.roll(cells, half, 1) if half else cells
        r2 = pltpu.roll(below, back, 1) if back else below
        both = jnp.where(lane < 64, r0, r1)
        for a in range(3):
            at = pl.ds(j * cell, cell)
            lhs1[at, a * 256 : a * 256 + 128] = both[a * rows : a * rows + cell].astype(BF16)
            lhs1[at, a * 256 + 128 : a * 256 + 256] = r2[a * rows : a * rows + cell].astype(BF16)
    loads[1].wait()
    w1 = w1_buf[...].reshape(768, chans)
    pre[...] = jnp.dot(lhs1[...], w1, preferred_element_type=F32)

    count = span * rows * cols
    own = [pl.ds(j * cell + 2 * rows, span * rows) for j in range(1, cols + 1)]
    total = jnp.zeros((1, chans), F32)
    for at in own:
        total = total + jnp.sum(pre[at, :], axis=0, keepdims=True)
    scaled = total * (1.0 / (count * group))
    parts = pieces(scaled, 0)
    local = jnp.sum(
        jnp.dot(parts.astype(BF16), gfull[...], preferred_element_type=F32), axis=0, keepdims=True
    )
    square = jnp.zeros((1, chans), F32)
    for at in own:
        off = pre[at, :] - local
        square = square + jnp.sum(off * off, axis=0, keepdims=True)
    both = parts + pieces(square, 3)
    sums = jnp.dot(both.astype(BF16), gsum[...], preferred_element_type=F32)
    ids = iota(sums.shape, 0)
    local_mean = jnp.sum(jnp.where(ids < 3, sums, 0.0), axis=0, keepdims=True)
    local_sq = jnp.sum(jnp.where(ids >= 3, sums, 0.0), axis=0, keepdims=True)
    stats[me] = jnp.concatenate([local_mean, local_sq], axis=0)

    def send_stats(k):
        pltpu.make_async_remote_copy(
            src_ref=stats.at[me],
            dst_ref=stats.at[me],
            send_sem=st_send,
            recv_sem=st_recv,
            device_id=peer_of(k),
            device_id_type=MESH,
        ).start()

    each_peer(send_stats)

    ups[2].wait()
    lax.fori_loop(2 * per, 3 * per, mix, 0)

    some = stats.at[pl.ds(0, peers - 1)]
    pltpu.make_async_copy(some, some, st_recv).wait()

    all_mean = jnp.zeros((1, 128), F32)
    for p in range(peers) if peers <= 16 else ():
        all_mean = all_mean + stats[p, 0:1, :]
    if peers > 16:
        all_mean = lax.fori_loop(0, peers, lambda p, t: t + stats[p, 0:1, :], all_mean)
    all_mean = all_mean * (1.0 / peers)

    def spread(p, acc):
        off = stats[p, 0:1, :] - all_mean
        return acc + stats[p, 1:2, :] + off * off * float(count * group)

    all_sq = jnp.zeros((1, 128), F32)
    if peers <= 16:
        for p in range(peers):
            all_sq = spread(p, all_sq)
    else:
        all_sq = lax.fori_loop(0, peers, spread, all_sq)
    inv = lax.rsqrt(all_sq * (1.0 / (peers * count * group)) + EPSILON)
    wide = jnp.dot(
        (pieces(all_mean, 0) + pieces(inv, 3)).astype(BF16), gexp[...], preferred_element_type=F32
    )
    ids = iota(wide.shape, 0)
    mean_c = jnp.sum(jnp.where(ids < 3, wide, 0.0), axis=0, keepdims=True)
    inv_c = jnp.sum(jnp.where(ids >= 3, wide, 0.0), axis=0, keepdims=True)
    loads[2].wait()
    loads[3].wait()
    scale_c = inv_c * gain_ref[...]
    shift_c = shift_ref[...]

    row_id = lax.rem(iota((cell, chans), 0), rows)
    early = iota((cell, chans), 0) < 2 * rows
    dead = early & (tm == 0)
    for j in range(act_c):
        y = (pre[pl.ds(j * cell, cell), :] - mean_c) * scale_c + shift_c
        act = y / (1.0 + jnp.exp(-y))
        gone = dead
        if j == 0:
            gone = gone | (q == 0)
        if j == act_c - 1:
            gone = gone | (q == n_tile - 1)
        act = jnp.where(gone, 0.0, act)
        above = jnp.where(row_id == 0, 0.0, pltpu.roll(act, 1, 0))
        below = jnp.where(row_id == rows - 1, 0.0, pltpu.roll(act, cell - 1, 0))
        for s, moved in enumerate((above, act, below)):
            for a in range(3):
                lhs2[s, pl.ds(j * span * rows, span * rows), a * chans : (a + 1) * chans] = moved[
                    a * rows : a * rows + span * rows
                ].astype(BF16)

    def weight(i, k):
        if i in (0, 3) and k in (0, 3):
            return raw[i - i // 3, k - k // 3]
        return mixed[i, k]

    many = cols * span * rows
    for ri in range(2):
        for cj in range(2):
            acc = jnp.zeros((many, out_ch), F32)
            for u in range(2):
                for v in range(2):
                    left = lhs2[ri + u, pl.ds((cj + v) * span * rows, many), :]
                    acc = acc + jnp.dot(
                        left, weight(2 * ri + u, 2 * cj + v), preferred_element_type=F32
                    )
            for j in range(cols):
                for t in range(span):
                    part = acc[(j * span + t) * rows : (j * span + t + 1) * rows]
                    first = t * 4 * rows * cols + ri * 2 * cols + 2 * j + cj
                    for h in range(out_ch // 128):
                        grid_out[h, pl.ds(first, rows, 4 * cols), :] = part[
                            :, h * 128 : (h + 1) * 128
                        ]
    for h in range(out_ch // 128):
        out_ref[0, :, 0, :, :, h * 128 : (h + 1) * 128] = (
            grid_out[h].reshape(span, 2 * rows, 2 * cols, 128).astype(BF16)
        )

    for dtm, dq, ds in moves:

        @pl.when(inside(dtm, dq))
        def _(dtm=dtm, dq=dq, ds=ds):
            lat_copy(dtm, dq, ds, tm, q, sect).wait_send()

    pltpu.make_async_copy(some, some, st_send).wait()


def shards(sizes, latents, in_weight, gn_gain, gn_shift, up_weight):
    n_tm, n_tile, n_sect = sizes
    clips, blk, _, rows, cols, lat_ch = latents.shape
    chans, out_ch = in_weight.shape[-1], up_weight.shape[-1]
    span = blk * n_sect
    cell = (span + 2) * rows
    act_c = cols + 2
    peers = n_tm * n_tile
    vmem = pl.BlockSpec(memory_space=pltpu.VMEM)
    return pl.pallas_call(
        functools.partial(kernel, sizes),
        out_shape=pltpu.VMEM((1, span, 1, 2 * rows, 2 * cols, out_ch), BF16),
        in_specs=[pl.BlockSpec(memory_space=pltpu.HBM)] * 5,
        out_specs=vmem,
        scratch_shapes=[
            pltpu.VMEM(latents.shape, BF16),
            pltpu.VMEM((1, chans), F32),
            pltpu.VMEM((1, chans), F32),
            pltpu.VMEM((3, clips, blk * rows, 128), BF16),
            pltpu.VMEM((2 * n_sect, 3, blk * rows, 128), BF16),
            pltpu.VMEM((3, 4, 4, in_weight.shape[3], chans), BF16),
            pltpu.VMEM((act_c * cell, 768), BF16),
            pltpu.VMEM((act_c * cell, chans), F32),
            pltpu.VMEM((chans, chans), BF16),
            pltpu.VMEM((chans, 128), BF16),
            pltpu.VMEM((128, chans), BF16),
            pltpu.VMEM((peers, 2, 128), F32),
            pltpu.VMEM((3, 3, 3 * chans, out_ch), BF16),
            pltpu.VMEM((4, 4, 3 * chans, out_ch), BF16),
            pltpu.VMEM((3, act_c * span * rows, 3 * chans), BF16),
            pltpu.VMEM((out_ch // 128, span * 4 * rows * cols, 128), F32),
            pltpu.SemaphoreType.DMA((4,)),
            pltpu.SemaphoreType.DMA((3,)),
            pltpu.SemaphoreType.DMA((2, 3, n_sect)),
            pltpu.SemaphoreType.DMA((2 * n_sect, 3)),
            pltpu.SemaphoreType.DMA,
            pltpu.SemaphoreType.DMA,
        ],
        compiler_params=pltpu.CompilerParams(
            collective_id=0, has_side_effects=True, vmem_limit_bytes=56 * 1024 * 1024
        ),
        cost_estimate=pl.CostEstimate(
            flops=2_500_000_000, bytes_accessed=8_000_000, transcendentals=300_000
        ),
    )(latents, in_weight, gn_gain.reshape(1, chans), gn_shift.reshape(1, chans), up_weight)


def solution(mesh):
    sizes = (mesh.shape["tm"], mesh.shape["tile"], mesh.shape["sect"])
    placed = (P(None, ("tm", "sect"), "tile", None, None, None), P(), P(), P(), P())
    return jax.shard_map(
        functools.partial(shards, sizes),
        mesh=mesh,
        in_specs=placed,
        out_specs=P("sect", "tm", "tile", None, None, None),
        check_vma=False,
    )
```

```python
import functools

import jax
import jax.numpy as jnp
from jax import lax
from jax.experimental import pallas as pl
from jax.experimental.pallas import tpu as pltpu
from jax.sharding import PartitionSpec as P

GROUPS = 32
EPSILON = 1e-06
MESH = pl.DeviceIdType.MESH
F32 = jnp.float32
BF16 = jnp.bfloat16


def iota(shape, dim):
    return lax.broadcasted_iota(jnp.int32, shape, dim)


def pieces(row, first, rows=8):
    high = row.astype(BF16).astype(F32)
    rest = row - high
    mid = rest.astype(BF16).astype(F32)
    low = rest - mid
    width = row.shape[-1]
    ids = iota((rows, width), 0)
    out = jnp.zeros((rows, width), F32)
    for k, part in enumerate((high, mid, low)):
        out = jnp.where(ids == first + k, jnp.broadcast_to(part, (rows, width)), out)
    return out


def kernel(
    sizes,
    lat_hbm,
    w1_hbm,
    gain_hbm,
    shift_hbm,
    up_ref,
    out_ref,
    lat_ref,
    gain_ref,
    shift_ref,
    sendbuf,
    latbuf,
    w1_buf,
    lhs1,
    pre,
    gfull,
    gsum,
    gexp,
    stats,
    raw,
    mixed,
    lhs2,
    grid_out,
    in_sem,
    up_sem,
    lat_send,
    lat_recv,
    st_send,
    st_recv,
):
    n_tm, n_tile, n_sect = sizes
    clips, blk, _, rows, cols, lat_ch = lat_hbm.shape
    chans = w1_hbm.shape[-1]
    out_ch = up_ref.shape[-1]
    group = chans // GROUPS
    span = blk * n_sect
    strip = blk * rows
    frames = 2 * span
    act_f = span + 2
    act_c = cols + 2
    cell = act_f * rows
    peers = n_tm * n_tile

    tm = lax.axis_index("tm")
    q = lax.axis_index("tile")
    sect = lax.axis_index("sect")
    me = tm * n_tile + q

    loads = [
        pltpu.make_async_copy(lat_hbm, lat_ref, in_sem.at[0]),
        pltpu.make_async_copy(w1_hbm, w1_buf.at[:, pl.ds(0, 3), pl.ds(0, 3)], in_sem.at[1]),
        pltpu.make_async_copy(gain_hbm, gain_ref, in_sem.at[2]),
        pltpu.make_async_copy(shift_hbm, shift_ref, in_sem.at[3]),
    ]
    loads[0].start()

    def inside(dtm, dq):
        return (tm + dtm >= 0) & (tm + dtm < n_tm) & (q + dq >= 0) & (q + dq < n_tile)

    barrier = pltpu.get_barrier_semaphore()

    def peer_of(k):
        other = lax.rem(me + k, peers)
        return (other // n_tile, lax.rem(other, n_tile), sect)

    far = sorted(range(n_tile), key=lambda d: -min(d, n_tile - d))
    order = [d + c * n_tile for d in far for c in range(n_tm - 1, -1, -1) if d + c]

    def each_peer(do):
        if peers <= 16:
            for k in order:
                do(k)
        else:

            def body(k, carry):
                do(k)
                return carry

            lax.fori_loop(1, peers, body, 0)

    def greet(k):
        pl.semaphore_signal(barrier, inc=1, device_id=peer_of(k), device_id_type=MESH)

    each_peer(greet)
    for ds in range(1, n_sect):
        for dtm in range(2):
            for dq in (-1, 0, 1):

                @pl.when(inside(-dtm, dq))
                def _(dtm=dtm, dq=dq, ds=ds):
                    pl.semaphore_signal(
                        barrier,
                        inc=1,
                        device_id=(tm - dtm, q + dq, lax.rem(sect + n_sect - ds, n_sect)),
                        device_id_type=MESH,
                    )

    for load in loads[1:]:
        load.start()
    ups = []
    for a in range(3):
        copy = pltpu.make_async_copy(
            up_ref.at[a], raw.at[:, :, pl.ds(a * chans, chans), :], up_sem.at[a]
        )
        copy.start()
        ups.append(copy)

    width = 128
    loads[0].wait()
    x = lat_ref[:, :, 0].astype(F32)
    placed = jnp.zeros((clips * strip, 3 * width), F32)
    for j in range(cols):
        col = x[:, :, :, j, :].reshape(clips * strip, lat_ch).astype(BF16)
        r = iota((lat_ch, 3 * width), 0)
        c = iota((lat_ch, 3 * width), 1)
        hit = (c == width + (j + 2) * lat_ch + r)
        if j >= cols - 2:
            hit = hit | (c == (j - cols + 2) * lat_ch + r)
        if j < 2:
            hit = hit | (c == 2 * width + (j + 2 + cols) * lat_ch + r)
        place = jnp.where(hit, 1.0, 0.0).astype(BF16)
        placed = placed + jnp.dot(col, place, preferred_element_type=F32)
    for pos in range(3):
        sendbuf[pos] = (
            placed[:, pos * width : (pos + 1) * width].astype(BF16).reshape(clips, strip, width)
        )

    targets = n_sect - 1
    steps_tm = jnp.where(tm + 1 < n_tm, 2, 1)
    steps_q = 1 + jnp.where(q > 0, 1, 0) + jnp.where(q + 1 < n_tile, 1, 0)
    pl.semaphore_wait(barrier, peers - 1 + targets * steps_tm * steps_q)

    def lat_copy(dtm, dq, ds, src_tm, src_q, src_sect):
        clip = lax.rem(src_sect + ds, n_sect)
        pos = 1 - dq
        slot = (1 - dtm) * n_sect + src_sect
        return pltpu.make_async_remote_copy(
            src_ref=sendbuf.at[pos, clip],
            dst_ref=latbuf.at[slot, pos],
            send_sem=lat_send.at[dtm, pos, ds],
            recv_sem=lat_recv.at[slot, pos],
            device_id=(src_tm + dtm, src_q + dq, clip),
            device_id_type=MESH,
        )

    moves = [
        (dtm, dq, ds)
        for ds in reversed(range(n_sect))
        for dq in (1, -1, 0)
        for dtm in (1, 0)
        if (dtm, dq, ds) != (0, 0, 0)
    ]
    for dtm, dq, ds in moves:

        @pl.when(inside(dtm, dq))
        def _(dtm=dtm, dq=dq, ds=ds):
            lat_copy(dtm, dq, ds, tm, q, sect).start()

    latbuf[n_sect + sect, 1] = sendbuf[1, sect]
    for dtm, dq, ds in moves:

        @pl.when(jnp.logical_not(inside(-dtm, -dq)))
        def _(dtm=dtm, dq=dq, ds=ds):
            slot = (1 - dtm) * n_sect + lax.rem(sect + n_sect - ds, n_sect)
            latbuf[slot, 1 - dq] = jnp.zeros((strip, width), BF16)

    w1_buf[:, 3] = jnp.zeros((3, 4, lat_ch, chans), BF16)
    w1_buf[:, 0:3, 3] = jnp.zeros((3, 3, lat_ch, chans), BF16)

    r = iota((chans, chans), 0)
    c = iota((chans, chans), 1)
    gfull[...] = jnp.where(r // group == c // group, 1.0, 0.0).astype(BF16)
    r = iota((chans, 128), 0)
    c = iota((chans, 128), 1)
    gsum[...] = jnp.where((r >= c * group) & (r < (c + 1) * group), 1.0, 0.0).astype(BF16)
    r = iota((128, chans), 0)
    c = iota((128, chans), 1)
    gexp[...] = jnp.where((c >= r * group) & (c < (r + 1) * group), 1.0, 0.0).astype(BF16)

    step = 16

    def mix(k, carry):
        at = pl.ds(pl.multiple_of(k * step, step), step)
        taps = [[raw[b, e, at, :].astype(F32) for e in range(3)] for b in range(3)]
        sums = [
            taps[0],
            [taps[1][e] + taps[2][e] for e in range(3)],
            [taps[0][e] + taps[1][e] for e in range(3)],
            taps[2],
        ]
        for i, row in enumerate(sums):
            if i in (1, 2):
                mixed[i, 0, at, :] = row[0].astype(BF16)
                mixed[i, 3, at, :] = row[2].astype(BF16)
            mixed[i, 1, at, :] = (row[1] + row[2]).astype(BF16)
            mixed[i, 2, at, :] = (row[0] + row[1]).astype(BF16)
        return carry

    per = chans // step
    for a in range(2):
        ups[a].wait()
        lax.fori_loop(a * per, (a + 1) * per, mix, 0)

    for dtm, dq, ds in moves:

        @pl.when(inside(-dtm, -dq))
        def _(dtm=dtm, dq=dq, ds=ds):
            src = lax.rem(sect + n_sect - ds, n_sect)
            lat_copy(dtm, dq, ds, tm - dtm, q - dq, src).wait_recv()

    cells = (
        latbuf[:, 0].astype(F32) + latbuf[:, 1].astype(F32) + latbuf[:, 2].astype(F32)
    ).reshape(frames * rows, width)
    row_id = lax.rem(iota((frames * rows, width), 0), rows)
    lane = iota((frames * rows, width), 1)
    above = jnp.where(row_id == 0, 0.0, pltpu.roll(cells, 1, 0))
    below = jnp.where(row_id == rows - 1, 0.0, pltpu.roll(cells, frames * rows - 1, 0))
    for j in range(act_c):
        back = (width - j * lat_ch) % width
        half = (width + 64 - j * lat_ch) % width
        r0 = pltpu.roll(above, back, 1) if back else above
        r1 = pltpu.roll(cells, half, 1) if half else cells
        r2 = pltpu.roll(below, back, 1) if back else below
        both = jnp.where(lane < 64, r0, r1)
        for a in range(3):
            at = pl.ds(j * cell, cell)
            lhs1[at, a * 256 : a * 256 + 128] = both[a * rows : a * rows + cell].astype(BF16)
            lhs1[at, a * 256 + 128 : a * 256 + 256] = r2[a * rows : a * rows + cell].astype(BF16)
    loads[1].wait()
    w1 = w1_buf[...].reshape(768, chans)
    pre[...] = jnp.dot(lhs1[...], w1, preferred_element_type=F32)

    count = span * rows * cols
    own = [pl.ds(j * cell + 2 * rows, span * rows) for j in range(1, cols + 1)]
    total = jnp.zeros((1, chans), F32)
    for at in own:
        total = total + jnp.sum(pre[at, :], axis=0, keepdims=True)
    scaled = total * (1.0 / (count * group))
    parts = pieces(scaled, 0)
    local = jnp.sum(
        jnp.dot(parts.astype(BF16), gfull[...], preferred_element_type=F32), axis=0, keepdims=True
    )
    square = jnp.zeros((1, chans), F32)
    for at in own:
        off = pre[at, :] - local
        square = square + jnp.sum(off * off, axis=0, keepdims=True)
    both = parts + pieces(square, 3)
    sums = jnp.dot(both.astype(BF16), gsum[...], preferred_element_type=F32)
    ids = iota(sums.shape, 0)
    local_mean = jnp.sum(jnp.where(ids < 3, sums, 0.0), axis=0, keepdims=True)
    local_sq = jnp.sum(jnp.where(ids >= 3, sums, 0.0), axis=0, keepdims=True)
    stats[me] = jnp.concatenate([local_mean, local_sq], axis=0)

    def send_stats(k):
        pltpu.make_async_remote_copy(
            src_ref=stats.at[me],
            dst_ref=stats.at[me],
            send_sem=st_send,
            recv_sem=st_recv,
            device_id=peer_of(k),
            device_id_type=MESH,
        ).start()

    each_peer(send_stats)

    ups[2].wait()
    lax.fori_loop(2 * per, 3 * per, mix, 0)

    some = stats.at[pl.ds(0, peers - 1)]
    pltpu.make_async_copy(some, some, st_recv).wait()

    all_mean = jnp.zeros((1, 128), F32)
    for p in range(peers) if peers <= 16 else ():
        all_mean = all_mean + stats[p, 0:1, :]
    if peers > 16:
        all_mean = lax.fori_loop(0, peers, lambda p, t: t + stats[p, 0:1, :], all_mean)
    all_mean = all_mean * (1.0 / peers)

    def spread(p, acc):
        off = stats[p, 0:1, :] - all_mean
        return acc + stats[p, 1:2, :] + off * off * float(count * group)

    all_sq = jnp.zeros((1, 128), F32)
    if peers <= 16:
        for p in range(peers):
            all_sq = spread(p, all_sq)
    else:
        all_sq = lax.fori_loop(0, peers, spread, all_sq)
    inv = lax.rsqrt(all_sq * (1.0 / (peers * count * group)) + EPSILON)
    wide = jnp.dot(
        (pieces(all_mean, 0) + pieces(inv, 3)).astype(BF16), gexp[...], preferred_element_type=F32
    )
    ids = iota(wide.shape, 0)
    mean_c = jnp.sum(jnp.where(ids < 3, wide, 0.0), axis=0, keepdims=True)
    inv_c = jnp.sum(jnp.where(ids >= 3, wide, 0.0), axis=0, keepdims=True)
    loads[2].wait()
    loads[3].wait()
    scale_c = inv_c * gain_ref[...]
    shift_c = shift_ref[...]

    row_id = lax.rem(iota((cell, chans), 0), rows)
    early = iota((cell, chans), 0) < 2 * rows
    dead = early & (tm == 0)
    for j in range(act_c):
        y = (pre[pl.ds(j * cell, cell), :] - mean_c) * scale_c + shift_c
        act = y / (1.0 + jnp.exp(-y))
        gone = dead
        if j == 0:
            gone = gone | (q == 0)
        if j == act_c - 1:
            gone = gone | (q == n_tile - 1)
        act = jnp.where(gone, 0.0, act)
        above = jnp.where(row_id == 0, 0.0, pltpu.roll(act, 1, 0))
        below = jnp.where(row_id == rows - 1, 0.0, pltpu.roll(act, cell - 1, 0))
        for s, moved in enumerate((above, act, below)):
            for a in range(3):
                lhs2[s, pl.ds(j * span * rows, span * rows), a * chans : (a + 1) * chans] = moved[
                    a * rows : a * rows + span * rows
                ].astype(BF16)

    def weight(i, k):
        if i in (0, 3) and k in (0, 3):
            return raw[i - i // 3, k - k // 3]
        return mixed[i, k]

    many = cols * span * rows
    for ri in range(2):
        for cj in range(2):
            acc = jnp.zeros((many, out_ch), F32)
            for u in range(2):
                for v in range(2):
                    left = lhs2[ri + u, pl.ds((cj + v) * span * rows, many), :]
                    acc = acc + jnp.dot(
                        left, weight(2 * ri + u, 2 * cj + v), preferred_element_type=F32
                    )
            for j in range(cols):
                for t in range(span):
                    part = acc[(j * span + t) * rows : (j * span + t + 1) * rows]
                    first = t * 4 * rows * cols + ri * 2 * cols + 2 * j + cj
                    for h in range(out_ch // 128):
                        grid_out[h, pl.ds(first, rows, 4 * cols), :] = part[
                            :, h * 128 : (h + 1) * 128
                        ]
        for h in range(out_ch // 128):
            for t in range(span):
                for i in range(rows):
                    first = ((t * rows + i) * 2 + ri) * 2 * cols
                    out_ref[0, t, 0, 2 * i + ri, :, h * 128 : (h + 1) * 128] = grid_out[
                        h, first : first + 2 * cols, :
                    ].astype(BF16)

    for dtm, dq, ds in moves:

        @pl.when(inside(dtm, dq))
        def _(dtm=dtm, dq=dq, ds=ds):
            lat_copy(dtm, dq, ds, tm, q, sect).wait_send()

    pltpu.make_async_copy(some, some, st_send).wait()


def shards(sizes, latents, in_weight, gn_gain, gn_shift, up_weight):
    n_tm, n_tile, n_sect = sizes
    clips, blk, _, rows, cols, lat_ch = latents.shape
    chans, out_ch = in_weight.shape[-1], up_weight.shape[-1]
    span = blk * n_sect
    cell = (span + 2) * rows
    act_c = cols + 2
    peers = n_tm * n_tile
    vmem = pl.BlockSpec(memory_space=pltpu.VMEM)
    return pl.pallas_call(
        functools.partial(kernel, sizes),
        out_shape=pltpu.VMEM((1, span, 1, 2 * rows, 2 * cols, out_ch), BF16),
        in_specs=[pl.BlockSpec(memory_space=pltpu.HBM)] * 5,
        out_specs=vmem,
        scratch_shapes=[
            pltpu.VMEM(latents.shape, BF16),
            pltpu.VMEM((1, chans), F32),
            pltpu.VMEM((1, chans), F32),
            pltpu.VMEM((3, clips, blk * rows, 128), BF16),
            pltpu.VMEM((2 * n_sect, 3, blk * rows, 128), BF16),
            pltpu.VMEM((3, 4, 4, in_weight.shape[3], chans), BF16),
            pltpu.VMEM((act_c * cell, 768), BF16),
            pltpu.VMEM((act_c * cell, chans), F32),
            pltpu.VMEM((chans, chans), BF16),
            pltpu.VMEM((chans, 128), BF16),
            pltpu.VMEM((128, chans), BF16),
            pltpu.VMEM((peers, 2, 128), F32),
            pltpu.VMEM((3, 3, 3 * chans, out_ch), BF16),
            pltpu.VMEM((4, 4, 3 * chans, out_ch), BF16),
            pltpu.VMEM((3, act_c * span * rows, 3 * chans), BF16),
            pltpu.VMEM((out_ch // 128, span * 4 * rows * cols, 128), F32),
            pltpu.SemaphoreType.DMA((4,)),
            pltpu.SemaphoreType.DMA((3,)),
            pltpu.SemaphoreType.DMA((2, 3, n_sect)),
            pltpu.SemaphoreType.DMA((2 * n_sect, 3)),
            pltpu.SemaphoreType.DMA,
            pltpu.SemaphoreType.DMA,
        ],
        compiler_params=pltpu.CompilerParams(
            collective_id=0, has_side_effects=True, vmem_limit_bytes=56 * 1024 * 1024
        ),
        cost_estimate=pl.CostEstimate(
            flops=2_500_000_000, bytes_accessed=8_000_000, transcendentals=300_000
        ),
    )(latents, in_weight, gn_gain.reshape(1, chans), gn_shift.reshape(1, chans), up_weight)


def solution(mesh):
    sizes = (mesh.shape["tm"], mesh.shape["tile"], mesh.shape["sect"])
    placed = (P(None, ("tm", "sect"), "tile", None, None, None), P(), P(), P(), P())
    return jax.shard_map(
        functools.partial(shards, sizes),
        mesh=mesh,
        in_specs=placed,
        out_specs=P("sect", "tm", "tile", None, None, None),
        check_vma=False,
    )
```
